256 devices in a mesh: dp: 16 (over x_lo, z), expert: 16 (over y, x_hi, core).
Axes of the slice: x: 4 (x_hi: 2, x_lo: 2; x = x_hi * 2 + x_lo), y: 4, z: 8, core: 2. Of those that a mesh axis runs over, the one named last changes fastest.
Arguments:
- images: bfloat16 [512, 256, 768], P(('dp', 'expert')), may hold values from -64 to 64
- out_grad: bfloat16 [512, 256, 768], P(('dp', 'expert')), may hold values from -6 to 6
- router: bfloat16 [768, 128], replicated, may hold values from -0.14505926 to 0.14505926
- w_in: bfloat16 [16, 768, 3072], P('expert'), may hold values from -0.21875 to 0.21875
- w_out: bfloat16 [16, 3072, 768], P('expert'), may hold values from -0.109375 to 0.109375
Outputs:
- image_grad: bfloat16 [512, 256, 768], P(('dp', 'expert'))
- router_grad: float32 [768, 128], replicated
- w_in_grad: bfloat16 [16, 768, 3072], P('expert', 'dp')
- w_out_grad: bfloat16 [16, 3072, 768], P('expert', 'dp')
The draws below stay inside these ranges and needn't reach their ends.
All inputs are finite; a program needn't handle non-finite values.
Results may differ from the reference program's by a relative error of at most 0.023.
Values may be sent and summed in bfloat16 or wider, within the bound.
A program may use at most 64 MiB of HBM per device.

```python
import math
import jax
import jax.numpy as jnp
from jax import lax

D = 768
H = 3072
M = 256
SPE = 8
EXPERTS = 16
SLOTS = 128
IMAGES = 512
N_DP = 16


def shared_router(key):
    return jnp.clip(jax.random.normal(key, (D, SLOTS), jnp.float32), -4.0, 4.0) / math.sqrt(D)


def draw_router(key, part):
    base = shared_router(key)
    return base.astype(jnp.bfloat16)


def draw_images(key, part):
    key = jax.random.fold_in(key, 11)
    key_base = jax.random.fold_in(key, 0)
    values = jnp.clip(jax.random.normal(key_base, (IMAGES, M, D), jnp.float32), -6.0, 6.0)
    return jnp.clip(values, -64.0, 64.0).astype(jnp.bfloat16)


def levels(own_key, shape, cuts, smallest, high):
    gain = 1.0
    for axis_at, blocks in cuts:
        steps = jax.random.uniform(jax.random.fold_in(jax.random.fold_in(own_key, 6), axis_at), (blocks,), jnp.float32, smallest / len(cuts), high / len(cuts))
        gain = gain * jnp.repeat(jnp.exp(steps), shape[axis_at] // blocks).reshape((-1,) + (1,) * (len(shape) - 1 - axis_at))
    return gain


def centred(rng, extent, spread, bound, shards=(), dtype=jnp.bfloat16):
    values = spread * jax.random.normal(rng, extent, jnp.float32)
    if shards:
        values = values * levels(rng, extent, shards, -0.22, 0.18)
    return jnp.clip(values, -bound, bound).astype(dtype)


def setup_inputs(seed: int = 0) -> dict:
    key_of = jax.random.split(jax.random.key(seed), 6)
    images = draw_images(jax.random.fold_in(key_of[5], 71), 0)
    out_grad = centred(key_of[1], (IMAGES, M, D), 1.0, 6.0, ((0, 256),))
    router = draw_router(jax.random.fold_in(key_of[5], 71), 0)
    w_in = centred(key_of[3], (EXPERTS, D, H), D ** -0.5, 0.21875, ((0, 16),))
    w_out = centred(key_of[4], (EXPERTS, H, D), H ** -0.5, 0.109375, ((0, 16),))
    return dict(images=images, out_grad=out_grad, router=router, w_in=w_in, w_out=w_out)


def contract_last(left, right):
    return lax.dot_general(left, right, (((1,), (1,)), ((), ())), preferred_element_type=jnp.float32)

def grouped_sum(left, right):
    left_groups = left.astype(jnp.float32).reshape(N_DP, -1, left.shape[1])
    right_groups = right.astype(jnp.float32).reshape(N_DP, -1, right.shape[1])
    partial_sums = jnp.einsum('gri,grj->gij', left_groups, right_groups)
    rounded = lax.optimization_barrier(partial_sums.astype(jnp.bfloat16))
    return lax.optimization_barrier(jnp.sum(rounded.astype(jnp.float32), axis=0))

def expert_pass(expert_rows, grad_rows, weight_in, weight_out):
    pre_act = jnp.dot(expert_rows, weight_in, preferred_element_type=jnp.float32)
    hidden_act, backward = jax.vjp(jax.nn.gelu, pre_act)
    hidden_bf = hidden_act.astype(jnp.bfloat16)
    slot_out = jnp.dot(hidden_bf, weight_out, preferred_element_type=jnp.float32).astype(jnp.bfloat16)
    delta_hidden = contract_last(grad_rows, weight_out)
    delta_act = backward(delta_hidden)[0].astype(jnp.bfloat16)
    slot_dx = contract_last(delta_act, weight_in).astype(jnp.bfloat16)
    grad_first = grouped_sum(expert_rows, delta_act)
    grad_second = grouped_sum(hidden_bf, grad_rows)
    return (slot_out, slot_dx, grad_first, grad_second)

def reference(images, out_grad, router, w_in, w_out):
    image_f32 = images.astype(jnp.float32)
    grad_f32 = out_grad.astype(jnp.float32)
    router_f32 = router.astype(jnp.float32)
    logits = jnp.einsum('bmd,ds->bms', image_f32, router_f32)
    dispatch = jax.nn.softmax(logits, axis=1)
    combine = jax.nn.softmax(logits, axis=2)
    disp_bf = dispatch.astype(jnp.bfloat16).astype(jnp.float32)
    comb_bf = combine.astype(jnp.bfloat16).astype(jnp.float32)
    slot_in = jnp.einsum('bms,bmd->bsd', disp_bf, image_f32).astype(jnp.bfloat16)
    slot_grad = jnp.einsum('bms,bmd->bsd', comb_bf, grad_f32).astype(jnp.bfloat16)

    def group(array):
        return array.reshape(IMAGES, EXPERTS, SPE, D).transpose(1, 0, 2, 3).reshape(EXPERTS, IMAGES * SPE, D)

    def ungroup(array):
        return array.reshape(EXPERTS, IMAGES, SPE, D).transpose(1, 0, 2, 3).reshape(IMAGES, SLOTS, D)
    slot_out, slot_dx, grad_first, grad_second = lax.map(lambda items: expert_pass(items[0], items[1], items[2], items[3]), (group(slot_in), group(slot_grad), w_in, w_out))
    slot_out = ungroup(slot_out).astype(jnp.float32)
    slot_dx = ungroup(slot_dx).astype(jnp.float32)
    dcomb = jnp.einsum('bmd,bsd->bms', grad_f32, slot_out)
    ddisp = jnp.einsum('bmd,bsd->bms', image_f32, slot_dx)
    dlogits = combine * (dcomb - lax.optimization_barrier(jnp.sum(combine * dcomb, axis=2, keepdims=True)))
    dlogits = dlogits + dispatch * (ddisp - lax.optimization_barrier(jnp.sum(dispatch * ddisp, axis=1, keepdims=True)))
    dlogits = dlogits.astype(jnp.bfloat16).astype(jnp.float32)
    image_grad = jnp.einsum('bms,bsd->bmd', disp_bf, slot_dx) + jnp.einsum('bms,ds->bmd', dlogits, router_f32)
    router_grad = jnp.einsum('bmd,bms->ds', image_f32, dlogits)
    return (image_grad.astype(jnp.bfloat16), router_grad, grad_first.astype(jnp.bfloat16), grad_second.astype(jnp.bfloat16))
```

```python
import math

import jax
import jax.numpy as jnp
from jax import lax
from jax.experimental import pallas as pl
from jax.experimental.pallas import tpu as pltpu
from jax.sharding import PartitionSpec as P

MESH = pl.DeviceIdType.MESH
BF = jnp.bfloat16
F32 = jnp.float32

D = 768
H = 3072
M = 256
S = 128
E = 16
NZ = 8
PER = 2
SPE = 8
BLK = PER * SPE
ROWS = E * BLK
TILE = 512
NT = H // TILE
HALF_T = NT // 2
CH_IN = D // (2 * NZ)
CH_OUT = H // (2 * NZ)
C0 = math.sqrt(2.0 / math.pi)
C1 = 0.044715


def dot(a, b, ca, cb):
    return lax.dot_general(a, b, (((ca,), (cb,)), ((), ())), preferred_element_type=F32)


def kernel(
    images, out_grad, router, w_in_hbm, w_out_hbm,
    image_grad, router_grad_t, w_in_share, w_out_share,
    w_in, w_out, disp, comb, sb_in, sb_grad, x_rows, g_rows,
    hid, gp, da, xt, gw_out, gw_in,
    ro_half, ro_full, ri_half, ri_full,
    so_send, dx_send, so_home, dx_home,
    rpart, r_a, r_b1, b_mine, r_b2, c_mine, r_c,
    w_sem, a2a_send, a2a_recv, rs_send, rs_recv, ar_send, ar_recv, loc_sem,
):
    d = lax.axis_index("dp")
    e = lax.axis_index("expert")
    pair = d // NZ
    z = d % NZ
    other_dp = (1 - pair) * NZ + z

    def zdev(k):
        return (pair * NZ + (z + k) % NZ, e)

    def w_copy(k):
        t = (HALF_T * pair + k) % NT
        return (
            pltpu.make_async_copy(w_in_hbm.at[:, pl.ds(pl.multiple_of(t * TILE, TILE), TILE)], w_in.at[k], w_sem.at[0, k]),
            pltpu.make_async_copy(w_out_hbm.at[pl.ds(pl.multiple_of(t * TILE, TILE), TILE), :], w_out.at[k], w_sem.at[1, k]),
        )

    for k in range(NT):
        for c in w_copy(k):
            c.start()

    barrier = pltpu.get_barrier_semaphore()

    def greet(k, _):
        to = (e + k) % E
        pl.semaphore_signal(barrier, inc=1, device_id=(other_dp, to), device_id_type=MESH)
        return 0

    lax.fori_loop(0, E, greet, 0)

    def greet_own(k, _):
        pl.semaphore_signal(barrier, inc=1, device_id=(d, (e + k) % E), device_id_type=MESH)
        return 0

    lax.fori_loop(1, E, greet_own, 0)
    for k in range(1, NZ):
        pl.semaphore_signal(barrier, inc=1, device_id=zdev(k), device_id_type=MESH)

    def spread(src, dst, n):
        pltpu.make_async_copy(src.at[e], dst.at[0, e], a2a_recv.at[n]).start()

        def far(k, _):
            to = (e + k) % E
            pltpu.make_async_remote_copy(
                src_ref=src.at[to], dst_ref=dst.at[1, e],
                send_sem=a2a_send.at[n, 1], recv_sem=a2a_recv.at[n],
                device_id=(other_dp, to), device_id_type=MESH,
            ).start()
            return 0

        def near(k, _):
            to = (e + k) % E
            pltpu.make_async_remote_copy(
                src_ref=src.at[to], dst_ref=dst.at[0, e],
                send_sem=a2a_send.at[n, 0], recv_sem=a2a_recv.at[n],
                device_id=(d, to), device_id_type=MESH,
            ).start()
            return far(k, 0)

        far(0, 0)
        lax.fori_loop(1, E, near, 0)

    def wait_bytes(ref, sem):
        pltpu.make_async_copy(ref, ref, sem).wait()

    def back(src, dst, n):
        pltpu.make_async_copy(src.at[e], dst.at[e], a2a_recv.at[n]).start()

        def near(k, _):
            to = (e + k) % E
            pltpu.make_async_remote_copy(
                src_ref=src.at[to], dst_ref=dst.at[e],
                send_sem=a2a_send.at[n, 0], recv_sem=a2a_recv.at[n],
                device_id=(d, to), device_id_type=MESH,
            ).start()
            return 0

        lax.fori_loop(1, E, near, 0)

    def pack(parts):
        parts = [p.reshape(E, SPE, D) for p in parts]
        return jnp.concatenate(parts, axis=1).astype(BF)

    parts = []
    logits = []
    for i in range(PER):
        lg = dot(images[i], router[...], 1, 0)
        logits.append(lg)
        ex = jnp.exp(lg - jnp.max(lg, axis=0, keepdims=True))
        p = ex / jnp.sum(ex, axis=0, keepdims=True)
        disp[i] = p
        parts.append(dot(p.astype(BF), images[i], 0, 0))
    sb_in[...] = pack(parts)
    pl.semaphore_wait(barrier, 2 * E - 1 + NZ - 1)
    spread(sb_in, x_rows, 0)
    parts = []
    for i in range(PER):
        lg = logits[i]
        ex = jnp.exp(lg - jnp.max(lg, axis=1, keepdims=True))
        p = ex / jnp.sum(ex, axis=1, keepdims=True)
        comb[i] = p
        parts.append(dot(p.astype(BF), out_grad[i], 0, 0))
    sb_grad[...] = pack(parts)
    spread(sb_grad, g_rows, 1)

    def xs():
        return x_rows[...].reshape(2 * ROWS, D)

    def gs():
        return g_rows[...].reshape(2 * ROWS, D)

    def forward(k, _):
        pre = dot(xs(), w_in[k], 1, 0)
        sq = pre * pre
        t = jnp.tanh(pre * (C0 + (C0 * C1) * sq))
        half = 0.5 * pre
        hid[k] = (half + half * t).astype(BF)
        gp[k] = (0.5 + 0.5 * t) + half * ((1.0 - t * t) * (C0 + (3.0 * C0 * C1) * sq))
        return 0

    def backward(k, _):
        dh = dot(gs(), w_out[k], 1, 1)
        da[k] = (dh * gp[k]).astype(BF)
        return 0

    def grad_out(k, _):
        g = dot(hid[k], gs(), 0, 0)
        gw_out[pl.ds(pl.multiple_of(k * TILE, TILE), TILE), :] = g.astype(BF)
        return 0

    def grad_in(k, _):
        g = dot(xt[...], da[k], 1, 0)
        gw_in[:, k] = g.reshape(NZ, CH_IN, TILE).astype(BF)
        return 0

    def rs_copy(which, way, step):
        c = (z + 5 - step) % NZ if way == 0 else (z + 3 + step) % NZ
        if which == 0:
            if step == 1:
                half = CH_OUT // 2
                src = gw_out.at[pl.ds(pl.multiple_of(c * CH_OUT + way * half, 16), half), :]
                dst = ro_half.at[way]
            else:
                src = gw_out.at[pl.ds(pl.multiple_of(c * CH_OUT, 16), CH_OUT), :]
                dst = ro_full.at[way, step - 2]
        else:
            if step == 1:
                src = gw_in.at[c, pl.ds(way * HALF_T, HALF_T)]
                dst = ri_half.at[way]
            else:
                src = gw_in.at[c]
                dst = ri_full.at[way, step - 2]
        return pltpu.make_async_remote_copy(
            src_ref=src, dst_ref=dst,
            send_sem=rs_send.at[which, way, step - 1], recv_sem=rs_recv.at[which, way, step - 1],
            device_id=zdev(1 if way == 0 else NZ - 1), device_id_type=MESH,
        )

    def rs_start(which, step):
        for way in range(2):
            rs_copy(which, way, step).start()

    def rs_next(which, step):
        for way in range(2):
            rs_copy(which, way, step).wait_recv()
            c = (z + 4 - step) % NZ if way == 0 else (z + 4 + step) % NZ
            if which == 0:
                if step == 1:
                    half = CH_OUT // 2
                    rows = pl.ds(pl.multiple_of(c * CH_OUT + way * half, 16), half)
                    got = ro_half[way]
                else:
                    rows = pl.ds(pl.multiple_of(c * CH_OUT, 16), CH_OUT)
                    got = ro_full[way, step - 2]
                gw_out[rows, :] = (gw_out[rows, :].astype(F32) + got.astype(F32)).astype(BF)
            else:
                if step == 1:
                    ks = pl.ds(way * HALF_T, HALF_T)
                    gw_in[c, ks] = (gw_in[c, ks].astype(F32) + ri_half[way].astype(F32)).astype(BF)
                else:
                    gw_in[c] = (gw_in[c].astype(F32) + ri_full[way, step - 2].astype(F32)).astype(BF)
            rs_copy(which, way, step + 1).start()

    def rs_end(which):
        for way in range(2):
            rs_copy(which, way, 4).wait_recv()
        if which == 0:
            rows = pl.ds(pl.multiple_of(z * CH_OUT, 16), CH_OUT)
            total = gw_out[rows, :].astype(F32) + ro_full[0, 2].astype(F32) + ro_full[1, 2].astype(F32)
            w_out_share[...] = total.astype(BF)
        else:
            for k in range(NT):
                t = (HALF_T * pair + k) % NT
                total = gw_in[z, k].astype(F32) + ri_full[0, 2, k].astype(F32) + ri_full[1, 2, k].astype(F32)
                w_in_share[:, pl.ds(pl.multiple_of(t * TILE, TILE), TILE)] = total.astype(BF)

    wait_bytes(x_rows, a2a_recv.at[0])
    for k in range(NT):
        w_copy(k)[0].wait()
    lax.fori_loop(0, HALF_T, forward, 0)
    off = pl.ds(pl.multiple_of(pair * (D // 2), 128), D // 2)
    xt[...] = jnp.transpose(x_rows[:, :, :, off].reshape(2 * ROWS, D // 2))
    wait_bytes(g_rows, a2a_recv.at[1])
    for k in range(NT):
        w_copy(k)[1].wait()
    lax.fori_loop(0, HALF_T, grad_out, 0)
    rs_start(0, 1)
    lax.fori_loop(0, HALF_T, backward, 0)
    rs_next(0, 1)
    lax.fori_loop(HALF_T, NT, forward, 0)
    lax.fori_loop(HALF_T, NT, backward, 0)
    lax.fori_loop(0, NT, grad_in, 0)
    rs_start(1, 1)

    def slot_out(k, acc):
        return acc + dot(hid[k, :ROWS], w_out[k], 1, 0)

    def slot_dx(k, acc):
        return acc + dot(da[k, :ROWS], w_in[k], 1, 1)

    zero = jnp.zeros((ROWS, D), F32)
    so_send[...] = lax.fori_loop(0, NT, slot_out, zero).astype(BF).reshape(E, BLK, D)
    back(so_send, so_home, 2)
    dx_send[...] = lax.fori_loop(0, NT, slot_dx, zero).astype(BF).reshape(E, BLK, D)
    back(dx_send, dx_home, 3)
    rs_next(0, 2)
    rs_next(1, 1)

    def home(ref, i):
        return ref[...].astype(F32).reshape(E, PER, SPE, D)[:, i].reshape(S, D).astype(BF)

    wait_bytes(so_home, a2a_recv.at[2])
    first = []
    for i in range(PER):
        dc = dot(out_grad[i], home(so_home, i), 1, 1)
        cm = comb[i]
        first.append(cm * (dc - jnp.sum(cm * dc, axis=1, keepdims=True)))
    wait_bytes(dx_home, a2a_recv.at[3])
    total = jnp.zeros((S, D), F32)
    for i in range(PER):
        dx = home(dx_home, i)
        dd = dot(images[i], dx, 1, 1)
        dm = disp[i]
        dl = (first[i] + dm * (dd - jnp.sum(dm * dd, axis=0, keepdims=True))).astype(BF)
        total = total + dot(dl, images[i], 0, 0)
        image_grad[i] = (dot(dm.astype(BF), dx, 1, 0) + dot(dl, router[...], 1, 1)).astype(BF)
    rpart[...] = total.reshape(E, SPE, D)

    pltpu.make_async_copy(rpart.at[e], r_a.at[e], ar_recv.at[0]).start()

    def send_a(k, _):
        to = (e + k) % E
        pltpu.make_async_remote_copy(
            src_ref=rpart.at[to], dst_ref=r_a.at[e], send_sem=ar_send.at[0], recv_sem=ar_recv.at[0],
            device_id=(d, to), device_id_type=MESH,
        ).start()
        return 0

    lax.fori_loop(1, E, send_a, 0)
    rs_next(0, 3)
    rs_next(1, 2)
    wait_bytes(r_a, ar_recv.at[0])
    summed = jnp.sum(r_a[...], axis=0)
    b_mine[0] = summed[:, : D // 2]
    b_mine[1] = summed[:, D // 2:]
    b1 = pltpu.make_async_remote_copy(
        src_ref=b_mine.at[1 - pair], dst_ref=r_b1, send_sem=ar_send.at[1], recv_sem=ar_recv.at[1],
        device_id=(other_dp, e), device_id_type=MESH,
    )
    b1.start()
    b1.wait()
    c_mine[...] = b_mine[pair] + r_b1[...]
    b2_self = pltpu.make_async_copy(c_mine, r_b2.at[z], ar_recv.at[2])
    b2_self.start()
    for k in range(1, NZ):
        pltpu.make_async_remote_copy(
            src_ref=c_mine, dst_ref=r_b2.at[z], send_sem=ar_send.at[2], recv_sem=ar_recv.at[2],
            device_id=zdev(k), device_id_type=MESH,
        ).start()
    rs_next(1, 3)
    rs_end(0)
    wait_bytes(r_b2, ar_recv.at[2])
    wait_bytes(r_b2.at[pl.ds(0, NZ - 1)], ar_send.at[2])
    c_mine[...] = jnp.sum(r_b2[...], axis=0)
    pltpu.make_async_copy(c_mine, r_c.at[pair, e], ar_recv.at[3]).start()

    def send_c_far(k, _):
        pltpu.make_async_remote_copy(
            src_ref=c_mine, dst_ref=r_c.at[pair, e], send_sem=ar_send.at[3], recv_sem=ar_recv.at[3],
            device_id=(other_dp, (e + k) % E), device_id_type=MESH,
        ).start()
        return 0

    def send_c(k, _):
        pltpu.make_async_remote_copy(
            src_ref=c_mine, dst_ref=r_c.at[pair, e], send_sem=ar_send.at[4], recv_sem=ar_recv.at[3],
            device_id=(d, (e + k) % E), device_id_type=MESH,
        ).start()
        return send_c_far(k, 0)

    send_c_far(0, 0)
    lax.fori_loop(1, E, send_c, 0)
    rs_end(1)
    wait_bytes(r_c, ar_recv.at[3])
    for h in range(2):
        router_grad_t[:, h * (D // 2): (h + 1) * (D // 2)] = r_c[h].reshape(S, D // 2)

    for n in range(2):
        wait_bytes(sb_in.at[pl.ds(0, E - 1)], a2a_send.at[n, 0])
        wait_bytes(sb_in, a2a_send.at[n, 1])
    for n in range(2, 4):
        wait_bytes(so_send.at[pl.ds(0, E - 1)], a2a_send.at[n, 0])
    for which in range(2):
        for way in range(2):
            for step in range(1, 5):
                rs_copy(which, way, step).wait_send()
    wait_bytes(rpart.at[pl.ds(0, E - 1)], ar_send.at[0])
    wait_bytes(r_c.at[0], ar_send.at[3])
    wait_bytes(r_c.at[0, pl.ds(0, E - 1)], ar_send.at[4])


def local(images, out_grad, router, w_in, w_out):
    vm = pl.BlockSpec(memory_space=pltpu.VMEM)
    hbm = pl.BlockSpec(memory_space=pl.ANY)
    V = pltpu.VMEM
    image_grad, router_grad_t, w_in_share, w_out_share = pl.pallas_call(
        kernel,
        out_shape=(
            jax.ShapeDtypeStruct((PER, M, D), BF),
            jax.ShapeDtypeStruct((S, D), F32),
            jax.ShapeDtypeStruct((CH_IN, H), BF),
            jax.ShapeDtypeStruct((CH_OUT, D), BF),
        ),
        in_specs=[vm, vm, vm, hbm, hbm],
        out_specs=(vm, vm, vm, vm),
        scratch_shapes=[
            V((NT, D, TILE), BF), V((NT, TILE, D), BF),
            V((PER, M, S), F32), V((PER, M, S), F32),
            V((E, BLK, D), BF), V((E, BLK, D), BF),
            V((2, E, BLK, D), BF), V((2, E, BLK, D), BF),
            V((NT, 2 * ROWS, TILE), BF), V((NT, 2 * ROWS, TILE), F32), V((NT, 2 * ROWS, TILE), BF),
            V((D // 2, 2 * ROWS), BF),
            V((H // 2, D), BF), V((NZ, NT, CH_IN, TILE), BF),
            V((2, CH_OUT // 2, D), BF), V((2, 3, CH_OUT, D), BF),
            V((2, HALF_T, CH_IN, TILE), BF), V((2, 3, NT, CH_IN, TILE), BF),
            V((E, BLK, D), BF), V((E, BLK, D), BF), V((E, BLK, D), BF), V((E, BLK, D), BF),
            V((E, SPE, D), F32), V((E, SPE, D), F32),
            V((SPE, D // 2), F32), V((2, SPE, D // 2), F32), V((NZ, SPE, D // 2), F32), V((SPE, D // 2), F32),
            V((2, E, SPE, D // 2), F32),
            pltpu.SemaphoreType.DMA((2, NT)),
            pltpu.SemaphoreType.DMA((4, 2)), pltpu.SemaphoreType.DMA((4,)),
            pltpu.SemaphoreType.DMA((2, 2, 4)), pltpu.SemaphoreType.DMA((2, 2, 4)),
            pltpu.SemaphoreType.DMA((5,)), pltpu.SemaphoreType.DMA((4,)),
            pltpu.SemaphoreType.DMA((1,)),
        ],
        compiler_params=pltpu.CompilerParams(
            collective_id=0, has_side_effects=True, vmem_limit_bytes=60 * 1024 * 1024
        ),
    )(images, out_grad, router, w_in[0], w_out[0])
    return image_grad, router_grad_t.T, w_in_share[None], w_out_share[None]


def solution(mesh):
    return jax.shard_map(
        local,
        mesh=mesh,
        in_specs=(
            P(("dp", "expert"), None, None),
            P(("dp", "expert"), None, None),
            P(),
            P("expert", None, None),
            P("expert", None, None),
        ),
        out_specs=(
            P(("dp", "expert"), None, None),
            P(),
            P("expert", "dp", None),
            P("expert", "dp", None),
        ),
        check_vma=False,
    )
```

```python
import math

import jax
import jax.numpy as jnp
from jax import lax
from jax.experimental import pallas as pl
from jax.experimental.pallas import tpu as pltpu
from jax.sharding import PartitionSpec as P

MESH = pl.DeviceIdType.MESH
BF = jnp.bfloat16
F32 = jnp.float32

D = 768
H = 3072
M = 256
S = 128
E = 16
NZ = 8
PER = 2
SPE = 8
BLK = PER * SPE
ROWS = E * BLK
TILE = 768
NT = H // TILE
HALF_T = NT // 2
IN_FLIGHT = 4
CH_IN = D // (2 * NZ)
CH_OUT = H // (2 * NZ)
C0 = math.sqrt(2.0 / math.pi)
C1 = 0.044715


def dot(a, b, ca, cb):
    return lax.dot_general(a, b, (((ca,), (cb,)), ((), ())), preferred_element_type=F32)


def kernel(
    images_hbm, out_grad_hbm, router_hbm, w_in_hbm, w_out_hbm,
    image_grad_hbm, router_grad_hbm, w_in_share_hbm, w_out_share_hbm,
    images, out_grad, router, image_grad, router_grad_t, w_in_share, w_out_share,
    w_in, w_out, disp, comb, sb_in, sb_grad, x_rows, g_rows,
    hid, gp, da, xt, gw_out, gw_in,
    ro_half, ro_full, ri_half, ri_full,
    so_send, dx_send, so_home, dx_home,
    rpart, r_a, b_rows, r_b2, c_row, r_b3, c_mine, r_c,
    w_sem, io_sem, a2a_send, a2a_recv, rs_send, rs_recv, ar_send, ar_recv,
):
    d = lax.axis_index("dp")
    e = lax.axis_index("expert")
    pair = d // NZ
    z = d % NZ
    other_dp = (1 - pair) * NZ + z

    def zdev(k):
        return (pair * NZ + (z + k) % NZ, e)

    def zdev_other(k):
        return ((1 - pair) * NZ + (z + k) % NZ, e)

    barrier = pltpu.get_barrier_semaphore()

    def greet(k, _):
        pl.semaphore_signal(barrier, inc=1, device_id=(other_dp, (e + k) % E), device_id_type=MESH)
        return 0

    def greet_own(k, _):
        pl.semaphore_signal(barrier, inc=1, device_id=(d, (e + k) % E), device_id_type=MESH)
        return 0

    lax.fori_loop(0, E, greet, 0)
    lax.fori_loop(1, E, greet_own, 0)
    for k in range(1, NZ):
        pl.semaphore_signal(barrier, inc=1, device_id=zdev(k), device_id_type=MESH)
        pl.semaphore_signal(barrier, inc=1, device_id=zdev_other(k), device_id_type=MESH)

    inputs = [
        pltpu.make_async_copy(images_hbm, images, io_sem.at[0]),
        pltpu.make_async_copy(router_hbm, router, io_sem.at[1]),
        pltpu.make_async_copy(out_grad_hbm, out_grad, io_sem.at[2]),
    ]
    for c in inputs:
        c.start()

    def tile_of(k):
        return 2 * ((pair + k // 2) % 2) + (1 - z // 4 + k) % 2

    def w_in_copy(k):
        cols = pl.ds(pl.multiple_of(tile_of(k) * TILE, TILE), TILE)
        return pltpu.make_async_copy(w_in_hbm.at[:, cols], w_in.at[k], w_sem.at[0, k])

    def w_out_copy(k):
        rows = pl.ds(pl.multiple_of(tile_of(k) * TILE, TILE), TILE)
        return pltpu.make_async_copy(w_out_hbm.at[rows, :], w_out.at[k], w_sem.at[1, k])

    for k in range(NT):
        w_in_copy(k).start()
    for k in range(NT):
        w_out_copy(k).start()

    def spread(src, dst, n):
        pltpu.make_async_copy(src.at[e], dst.at[0, e], a2a_recv.at[n]).start()

        def far(k, _):
            to = (e + k) % E
            pltpu.make_async_remote_copy(
                src_ref=src.at[to], dst_ref=dst.at[1, e],
                send_sem=a2a_send.at[n, 1], recv_sem=a2a_recv.at[n + 4],
                device_id=(other_dp, to), device_id_type=MESH,
            ).start()
            return 0

        def both(k, _):
            to = (e + k) % E
            pltpu.make_async_remote_copy(
                src_ref=src.at[to], dst_ref=dst.at[0, e],
                send_sem=a2a_send.at[n, 0], recv_sem=a2a_recv.at[n],
                device_id=(d, to), device_id_type=MESH,
            ).start()
            return far(k, 0)

        far(0, 0)
        lax.fori_loop(1, E, both, 0)

    def wait_bytes(ref, sem):
        pltpu.make_async_copy(ref, ref, sem).wait()

    def back(src, dst, n):
        pltpu.make_async_copy(src.at[e], dst.at[e], a2a_recv.at[n]).start()

        def near(k, _):
            to = (e + k) % E
            pltpu.make_async_remote_copy(
                src_ref=src.at[to], dst_ref=dst.at[e],
                send_sem=a2a_send.at[n, 0], recv_sem=a2a_recv.at[n],
                device_id=(d, to), device_id_type=MESH,
            ).start()
            return 0

        lax.fori_loop(1, E, near, 0)

    def pack(parts):
        parts = [p.reshape(E, SPE, D) for p in parts]
        return jnp.concatenate(parts, axis=1).astype(BF)

    parts = []
    logits = []
    inputs[0].wait()
    inputs[1].wait()
    for i in range(PER):
        lg = dot(images[i], router[...], 1, 0)
        logits.append(lg)
        ex = jnp.exp(lg - jnp.max(lg, axis=0, keepdims=True))
        p = ex / jnp.sum(ex, axis=0, keepdims=True)
        disp[i] = p
        parts.append(dot(p.astype(BF), images[i], 0, 0))
    sb_in[...] = pack(parts)
    pl.semaphore_wait(barrier, 2 * E - 1 + 2 * (NZ - 1))
    spread(sb_in, x_rows, 0)
    inputs[2].wait()
    parts = []
    for i in range(PER):
        lg = logits[i]
        ex = jnp.exp(lg - jnp.max(lg, axis=1, keepdims=True))
        p = ex / jnp.sum(ex, axis=1, keepdims=True)
        comb[i] = p
        parts.append(dot(p.astype(BF), out_grad[i], 0, 0))
    sb_grad[...] = pack(parts)
    wait_bytes(sb_in.at[pl.ds(0, E - 1)], a2a_send.at[0, 0])
    wait_bytes(sb_in, a2a_send.at[0, 1])
    spread(sb_grad, g_rows, 1)

    def xs():
        return x_rows[...].reshape(2 * ROWS, D)

    def forward(k, _):
        w_in_copy(k).wait()
        pre = dot(xs(), w_in[k], 1, 0)
        sq = pre * pre
        t = jnp.tanh(pre * (C0 + (C0 * C1) * sq))
        half = 0.5 * pre
        hid[k] = (half + half * t).astype(BF)
        gp[k] = (0.5 + 0.5 * t) + half * ((1.0 - t * t) * (C0 + (3.0 * C0 * C1) * sq))
        return 0

    def grad_out(k):
        g = dot(hid[k], g_rows[...].reshape(2 * ROWS, D), 0, 0).astype(BF)
        gw_out[pl.ds(((1 - z // 4 + k) % 2) * (NZ // 2), NZ // 2)] = g.reshape(NZ // 2, CH_OUT, D)

    def backward(k, part):
        rows = pl.ds(part * ROWS, ROWS)
        dh = dot(g_rows[part].reshape(ROWS, D), w_out[k], 1, 1)
        da[k, rows] = (dh * gp[k, rows]).astype(BF)

    def backward_own(k, _):
        backward(k, 0)
        return 0

    def grad_in(k, _):
        backward(k, 1)
        g = dot(xt[...], da[k], 1, 0)
        gw_in[:, tile_of(k)] = g.reshape(NZ, CH_IN, TILE).astype(BF)
        return 0

    def piece(which, part, c, way=None):
        if which == 0:
            rows = CH_OUT // 2 if way is None else CH_OUT // 4
            return (c, pl.ds(part * (CH_OUT // 2) + (way or 0) * rows, rows))
        first = HALF_T * ((pair + part) % 2)
        return (c, pl.ds(first, HALF_T)) if way is None else (c, pl.ds(first + way, 1))

    def rs_copy(which, part, way, step):
        c = (z + 5 - step) % NZ if way == 0 else (z + 3 + step) % NZ
        mine, half, full = ((gw_out, ro_half, ro_full), (gw_in, ri_half, ri_full))[which]
        src = mine.at[piece(which, part, c, way if step == 1 else None)]
        dst = half.at[part, way] if step == 1 else full.at[part, way, step - 2]
        return pltpu.make_async_remote_copy(
            src_ref=src, dst_ref=dst,
            send_sem=rs_send.at[which, part, way, step - 1], recv_sem=rs_recv.at[which, part, way, step - 1],
            device_id=zdev(1 if way == 0 else NZ - 1), device_id_type=MESH,
        )

    sent = []

    def rs_send_on(which, part, way, step):
        n = len(sent) // 2 - IN_FLIGHT
        if n >= 0:
            rs_copy(*sent[2 * n + way]).wait_send()
        rs_copy(which, part, way, step).start()
        sent.append((which, part, way, step))

    def rs_start(which, part):
        for way in range(2):
            rs_send_on(which, part, way, 1)

    def rs_next(which, part, step):
        mine, half, full = ((gw_out, ro_half, ro_full), (gw_in, ri_half, ri_full))[which]
        for way in range(2):
            rs_copy(which, part, way, step).wait_recv()
            c = (z + 4 - step) % NZ if way == 0 else (z + 4 + step) % NZ
            here = piece(which, part, c, way if step == 1 else None)
            got = half[part, way] if step == 1 else full[part, way, step - 2]
            mine[here] = (mine[here].astype(F32) + got.astype(F32)).astype(BF)
            rs_send_on(which, part, way, step + 1)

    def rs_end(which, part):
        for way in range(2):
            rs_copy(which, part, way, 4).wait_recv()
        if which == 0:
            rows = slice(part * (CH_OUT // 2), (part + 1) * (CH_OUT // 2))
            got = ro_full[part, 0, 2].astype(F32) + ro_full[part, 1, 2].astype(F32)
            w_out_share[rows, :] = (gw_out[z, rows, :].astype(F32) + got).astype(BF)
        else:
            for n in range(HALF_T):
                t = HALF_T * ((pair + part) % 2) + n
                got = ri_full[part, 0, 2, n].astype(F32) + ri_full[part, 1, 2, n].astype(F32)
                cols = pl.ds(pl.multiple_of(t * TILE, TILE), TILE)
                w_in_share[:, cols] = (gw_in[z, t].astype(F32) + got).astype(BF)

    wait_bytes(x_rows.at[0], a2a_recv.at[0])
    wait_bytes(x_rows.at[1], a2a_recv.at[4])
    lax.fori_loop(0, NT, forward, 0)
    off = pl.ds(pl.multiple_of(pair * (D // 2), 128), D // 2)
    xt[...] = jnp.transpose(x_rows[:, :, :, off].reshape(2 * ROWS, D // 2))
    acc = None
    for k in range(NT):
        w_out_copy(k).wait()
        part = dot(hid[k, :ROWS], w_out[k], 1, 0)
        acc = part if acc is None else acc + part
    so_send[...] = acc.astype(BF).reshape(E, BLK, D)
    wait_bytes(g_rows.at[0], a2a_recv.at[1])
    wait_bytes(g_rows.at[1], a2a_recv.at[5])
    grad_out(0)
    rs_start(0, 0)
    rs_start(0, 1)
    back(so_send, so_home, 2)
    grad_out(1)
    lax.fori_loop(0, NT, backward_own, 0)
    acc = dot(da[0, :ROWS], w_in[0], 1, 1)
    for k in range(1, NT):
        acc = acc + dot(da[k, :ROWS], w_in[k], 1, 1)
    dx_send[...] = acc.astype(BF).reshape(E, BLK, D)
    back(dx_send, dx_home, 3)
    rs_next(0, 0, 1)
    rs_next(0, 1, 1)
    lax.fori_loop(0, HALF_T, grad_in, 0)
    rs_start(1, 0)
    lax.fori_loop(HALF_T, NT, grad_in, 0)
    rs_start(1, 1)
    rs_next(0, 0, 2)
    rs_next(1, 0, 1)

    def home(ref, i):
        return ref[...].astype(F32).reshape(E, PER, SPE, D)[:, i].reshape(S, D).astype(BF)

    wait_bytes(so_home, a2a_recv.at[2])
    first = []
    for i in range(PER):
        dc = dot(out_grad[i], home(so_home, i), 1, 1)
        cm = comb[i]
        first.append(cm * (dc - jnp.sum(cm * dc, axis=1, keepdims=True)))
    wait_bytes(dx_home, a2a_recv.at[3])
    total = jnp.zeros((S, D), F32)
    for i in range(PER):
        dx = home(dx_home, i)
        dd = dot(images[i], dx, 1, 1)
        dm = disp[i]
        dl = (first[i] + dm * (dd - jnp.sum(dm * dd, axis=0, keepdims=True))).astype(BF)
        total = total + dot(dl, images[i], 0, 0)
        image_grad[i] = (dot(dm.astype(BF), dx, 1, 0) + dot(dl, router[...], 1, 1)).astype(BF)
    rpart[...] = total.reshape(E, SPE, D)
    image_grad_out = pltpu.make_async_copy(image_grad, image_grad_hbm, io_sem.at[3])
    image_grad_out.start()

    pltpu.make_async_copy(rpart.at[e], r_a.at[e], ar_recv.at[0]).start()

    def send_a(k, _):
        to = (e + k) % E
        pltpu.make_async_remote_copy(
            src_ref=rpart.at[to], dst_ref=r_a.at[e], send_sem=ar_send.at[0], recv_sem=ar_recv.at[0],
            device_id=(d, to), device_id_type=MESH,
        ).start()
        return 0

    lax.fori_loop(1, E, send_a, 0)
    rs_next(1, 1, 1)
    rs_next(0, 1, 2)
    rs_next(1, 0, 2)
    wait_bytes(r_a, ar_recv.at[0])
    summed = jnp.sum(r_a[...], axis=0)
    for h in range(2):
        for r in range(NZ):
            b_rows[h, r] = summed[r:r + 1, h * (D // 2): (h + 1) * (D // 2)]
    pltpu.make_async_copy(b_rows.at[pair, z], r_b2.at[pair, z], ar_recv.at[2]).start()
    for k in range(NZ):
        to = (z + k) % NZ
        if k:
            pltpu.make_async_remote_copy(
                src_ref=b_rows.at[pair, to], dst_ref=r_b2.at[pair, z], send_sem=ar_send.at[2], recv_sem=ar_recv.at[2],
                device_id=zdev(k), device_id_type=MESH,
            ).start()
        pltpu.make_async_remote_copy(
            src_ref=b_rows.at[1 - pair, to], dst_ref=r_b2.at[pair, z], send_sem=ar_send.at[1], recv_sem=ar_recv.at[2],
            device_id=zdev_other(k), device_id_type=MESH,
        ).start()
    rs_next(1, 1, 2)
    wait_bytes(r_b2, ar_recv.at[2])
    c_row[0] = jnp.sum(r_b2[...].reshape(2 * NZ, 1, D // 2), axis=0)
    pltpu.make_async_copy(c_row.at[0], r_b3.at[z], ar_recv.at[4]).start()
    for k in range(1, NZ):
        pltpu.make_async_remote_copy(
            src_ref=c_row.at[0], dst_ref=r_b3.at[z], send_sem=ar_send.at[5], recv_sem=ar_recv.at[4],
            device_id=zdev(k), device_id_type=MESH,
        ).start()
    rs_next(0, 0, 3)
    wait_bytes(r_b3, ar_recv.at[4])
    for r in range(NZ):
        c_mine[r:r + 1, :] = r_b3[r]
    pltpu.make_async_copy(c_mine, r_c.at[pair, e], ar_recv.at[3]).start()

    def send_c_far(k, _):
        pltpu.make_async_remote_copy(
            src_ref=c_mine, dst_ref=r_c.at[pair, e], send_sem=ar_send.at[3], recv_sem=ar_recv.at[3],
            device_id=(other_dp, (e + k) % E), device_id_type=MESH,
        ).start()
        return 0

    def send_c(k, _):
        pltpu.make_async_remote_copy(
            src_ref=c_mine, dst_ref=r_c.at[pair, e], send_sem=ar_send.at[4], recv_sem=ar_recv.at[3],
            device_id=(d, (e + k) % E), device_id_type=MESH,
        ).start()
        return send_c_far(k, 0)

    send_c_far(0, 0)
    lax.fori_loop(1, E, send_c, 0)
    rs_next(0, 1, 3)
    rs_next(1, 0, 3)
    rs_next(1, 1, 3)
    outputs = [
        pltpu.make_async_copy(router_grad_t, router_grad_hbm, io_sem.at[4]),
        pltpu.make_async_copy(w_out_share, w_out_share_hbm, io_sem.at[5]),
        pltpu.make_async_copy(w_in_share, w_in_share_hbm, io_sem.at[6]),
    ]
    rs_end(0, 0)
    rs_end(0, 1)
    outputs[1].start()
    rs_end(1, 0)
    wait_bytes(r_c, ar_recv.at[3])
    for h in range(2):
        router_grad_t[:, h * (D // 2): (h + 1) * (D // 2)] = r_c[h].reshape(S, D // 2)
    outputs[0].start()
    rs_end(1, 1)
    outputs[2].start()

    wait_bytes(sb_grad.at[pl.ds(0, E - 1)], a2a_send.at[1, 0])
    wait_bytes(sb_grad, a2a_send.at[1, 1])
    for n in range(2, 4):
        wait_bytes(so_send.at[pl.ds(0, E - 1)], a2a_send.at[n, 0])
    for last in sent[-2 * IN_FLIGHT:]:
        rs_copy(*last).wait_send()
    wait_bytes(rpart.at[pl.ds(0, E - 1)], ar_send.at[0])
    wait_bytes(b_rows.at[0], ar_send.at[1])
    for n in (2, 5):
        wait_bytes(b_rows.at[0, pl.ds(0, NZ - 1)], ar_send.at[n])
    wait_bytes(r_c.at[0], ar_send.at[3])
    wait_bytes(r_c.at[0, pl.ds(0, E - 1)], ar_send.at[4])
    image_grad_out.wait()
    for c in outputs:
        c.wait()


def deliver(image_grad_in, router_grad_in, w_in_in, w_out_in, image_grad, router_grad, w_in_share, w_out_share,
            held, held_in, held_out, router_t, router_held, sem):
    steps = (
        (router_grad_in, router_t, None),
        (image_grad_in, held, image_grad),
        (w_in_in, held_in, w_in_share.at[0]),
        (w_out_in, held_out, w_out_share.at[0]),
    )
    first = [pltpu.make_async_copy(a, b, sem.at[0, n]) for n, (a, b, _) in enumerate(steps)]
    second = [
        pltpu.make_async_copy(router_held, router_grad, sem.at[1, 0]),
        *(pltpu.make_async_copy(b, c, sem.at[1, n + 1]) for n, (_, b, c) in enumerate(steps[1:])),
    ]
    for c in first:
        c.start()
    first[0].wait()
    router_held[...] = jnp.transpose(router_t[...])
    second[0].start()
    for c, after in zip(first[1:], second[1:]):
        c.wait()
        after.start()
    for c in second:
        c.wait()


def local(images, out_grad, router, w_in, w_out):
    hbm = pl.BlockSpec(memory_space=pltpu.HBM)
    V = pltpu.VMEM
    DMA = pltpu.SemaphoreType.DMA
    parts = pl.pallas_call(
        kernel,
        out_shape=(
            jax.ShapeDtypeStruct((PER, M, D), BF),
            jax.ShapeDtypeStruct((S, D), F32),
            jax.ShapeDtypeStruct((CH_IN, H), BF),
            jax.ShapeDtypeStruct((CH_OUT, D), BF),
        ),
        in_specs=[hbm] * 5,
        out_specs=(hbm,) * 4,
        scratch_shapes=[
            V((PER, M, D), BF), V((PER, M, D), BF), V((D, S), BF),
            V((PER, M, D), BF), V((S, D), F32), V((CH_IN, H), BF), V((CH_OUT, D), BF),
            V((NT, D, TILE), BF), V((NT, TILE, D), BF),
            V((PER, M, S), F32), V((PER, M, S), F32),
            V((E, BLK, D), BF), V((E, BLK, D), BF),
            V((2, E, BLK, D), BF), V((2, E, BLK, D), BF),
            V((NT, 2 * ROWS, TILE), BF), V((NT, 2 * ROWS, TILE), F32), V((NT, 2 * ROWS, TILE), BF),
            V((D // 2, 2 * ROWS), BF),
            V((NZ, CH_OUT, D), BF), V((NZ, NT, CH_IN, TILE), BF),
            V((2, 2, CH_OUT // 4, D), BF), V((2, 2, 3, CH_OUT // 2, D), BF),
            V((2, 2, 1, CH_IN, TILE), BF), V((2, 2, 3, HALF_T, CH_IN, TILE), BF),
            V((E, BLK, D), BF), V((E, BLK, D), BF), V((E, BLK, D), BF), V((E, BLK, D), BF),
            V((E, SPE, D), F32), V((E, SPE, D), F32),
            V((2, NZ, 1, D // 2), F32), V((2, NZ, 1, D // 2), F32),
            V((1, 1, D // 2), F32), V((NZ, 1, D // 2), F32), V((SPE, D // 2), F32),
            V((2, E, SPE, D // 2), F32),
            DMA((2, NT)), DMA((7,)),
            DMA((4, 2)), DMA((6,)),
            DMA((2, 2, 2, 4)), DMA((2, 2, 2, 4)),
            DMA((6,)), DMA((5,)),
        ],
        compiler_params=pltpu.CompilerParams(
            collective_id=0, has_side_effects=True, vmem_limit_bytes=60 * 1024 * 1024
        ),
    )(images, out_grad, router, w_in[0], w_out[0])
    return pl.pallas_call(
        deliver,
        out_shape=(
            jax.ShapeDtypeStruct((PER, M, D), BF),
            jax.ShapeDtypeStruct((D, S), F32),
            jax.ShapeDtypeStruct((1, CH_IN, H), BF),
            jax.ShapeDtypeStruct((1, CH_OUT, D), BF),
        ),
        in_specs=[hbm] * 4,
        out_specs=(hbm,) * 4,
        scratch_shapes=[
            V((PER, M, D), BF), V((CH_IN, H), BF), V((CH_OUT, D), BF), V((S, D), F32), V((D, S), F32), DMA((2, 4)),
        ],
        compiler_params=pltpu.CompilerParams(vmem_limit_bytes=60 * 1024 * 1024),
    )(*parts)


def solution(mesh):
    return jax.shard_map(
        local,
        mesh=mesh,
        in_specs=(
            P(("dp", "expert"), None, None),
            P(("dp", "expert"), None, None),
            P(),
            P("expert", None, None),
            P("expert", None, None),
        ),
        out_specs=(
            P(("dp", "expert"), None, None),
            P(),
            P("expert", "dp", None),
            P("expert", "dp", None),
        ),
        check_vma=False,
    )
```

```python
import math

import jax
import jax.numpy as jnp
from jax import lax
from jax.experimental import pallas as pl
from jax.experimental.pallas import tpu as pltpu
from jax.sharding import PartitionSpec as P

MESH = pl.DeviceIdType.MESH
BF = jnp.bfloat16
F32 = jnp.float32

D = 768
H = 3072
M = 256
S = 128
E = 16
NZ = 8
PER = 2
SPE = 8
BLK = PER * SPE
ROWS = E * BLK
TILE = 768
NT = H // TILE
HALF_T = NT // 2
GP = 3
GW = D // GP
IN_FLIGHT = 5
CH_IN = D // (2 * NZ)
CH_OUT = H // (2 * NZ)
C0 = math.sqrt(2.0 / math.pi)
C1 = 0.044715


def dot(a, b, ca, cb):
    return lax.dot_general(a, b, (((ca,), (cb,)), ((), ())), preferred_element_type=F32)


def kernel(
    images_hbm, out_grad_hbm, router_hbm, w_in_hbm, w_out_hbm,
    image_grad, router_grad, w_in_share, w_out_share,
    images, out_grad, router,
    w_in, w_out, disp, comb, sb_in, sb_grad, x_rows, g_rows,
    hid, hid_t, gp, da, xt, gw_out, gw_in,
    ro_half, ro_full, ri_half, ri_full,
    so_send, dx_send, so_home, dx_home,
    rpart, r_a, b_rows, r_b2, c_row, r_b3, c_mine, r_c,
    w_sem, io_sem, a2a_send, a2a_recv, rs_send, rs_recv, ar_send, ar_recv,
):
    d = lax.axis_index("dp")
    e = lax.axis_index("expert")
    pair = d // NZ
    z = d % NZ
    other_dp = (1 - pair) * NZ + z

    def zdev(k):
        return (pair * NZ + (z + k) % NZ, e)

    def zdev_other(k):
        return ((1 - pair) * NZ + (z + k) % NZ, e)

    barrier = pltpu.get_barrier_semaphore()

    def greet(k, _):
        pl.semaphore_signal(barrier, inc=1, device_id=(other_dp, (e + k) % E), device_id_type=MESH)
        return 0

    def greet_own(k, _):
        pl.semaphore_signal(barrier, inc=1, device_id=(d, (e + k) % E), device_id_type=MESH)
        return 0

    lax.fori_loop(0, E, greet, 0)
    lax.fori_loop(1, E, greet_own, 0)
    for k in range(1, NZ):
        pl.semaphore_signal(barrier, inc=1, device_id=zdev(k), device_id_type=MESH)
        pl.semaphore_signal(barrier, inc=1, device_id=zdev_other(k), device_id_type=MESH)

    inputs = [
        pltpu.make_async_copy(images_hbm, images, io_sem.at[0]),
        pltpu.make_async_copy(router_hbm, router, io_sem.at[1]),
        pltpu.make_async_copy(out_grad_hbm, out_grad, io_sem.at[2]),
    ]
    for c in inputs:
        c.start()

    def tile_of(k):
        return 2 * ((pair + k // 2) % 2) + (1 - z // 4 + k) % 2

    def w_in_copy(k):
        cols = pl.ds(pl.multiple_of(tile_of(k) * TILE, TILE), TILE)
        return pltpu.make_async_copy(w_in_hbm.at[:, cols], w_in.at[k], w_sem.at[0, k])

    def w_out_copy(k):
        rows = pl.ds(pl.multiple_of(tile_of(k) * TILE, TILE), TILE)
        return pltpu.make_async_copy(w_out_hbm.at[rows, :], w_out.at[k], w_sem.at[1, k])

    for k in range(NT):
        w_in_copy(k).start()
    for k in range(NT):
        w_out_copy(k).start()

    def spread(src, dst, n):
        pltpu.make_async_copy(src.at[e], dst.at[0, e], a2a_recv.at[n, 0]).start()

        def far(k, _):
            to = (e + k) % E
            pltpu.make_async_remote_copy(
                src_ref=src.at[to], dst_ref=dst.at[1, e],
                send_sem=a2a_send.at[n, 1], recv_sem=a2a_recv.at[n, 1],
                device_id=(other_dp, to), device_id_type=MESH,
            ).start()
            return 0

        def both(k, _):
            to = (e + k) % E
            pltpu.make_async_remote_copy(
                src_ref=src.at[to], dst_ref=dst.at[0, e],
                send_sem=a2a_send.at[n, 0], recv_sem=a2a_recv.at[n, 0],
                device_id=(d, to), device_id_type=MESH,
            ).start()
            return far(k, 0)

        far(0, 0)
        lax.fori_loop(1, E, both, 0)

    def has_left(src, n):
        wait_bytes(src.at[pl.ds(0, E - 1)], a2a_send.at[n, 0])
        wait_bytes(src, a2a_send.at[n, 1])

    def has_come(dst, n):
        wait_bytes(dst.at[0], a2a_recv.at[n, 0])
        wait_bytes(dst.at[1], a2a_recv.at[n, 1])

    def wait_bytes(ref, sem):
        pltpu.make_async_copy(ref, ref, sem).wait()

    def back(src, dst, n):
        pltpu.make_async_copy(src.at[e], dst.at[e], a2a_recv.at[n, 0]).start()

        def near(k, _):
            to = (e + k) % E
            pltpu.make_async_remote_copy(
                src_ref=src.at[to], dst_ref=dst.at[e],
                send_sem=a2a_send.at[n, 0], recv_sem=a2a_recv.at[n, 0],
                device_id=(d, to), device_id_type=MESH,
            ).start()
            return 0

        lax.fori_loop(1, E, near, 0)

    def pack(parts):
        parts = [p.reshape(E, SPE, D) for p in parts]
        return jnp.concatenate(parts, axis=1).astype(BF)

    parts = []
    logits = []
    inputs[0].wait()
    inputs[1].wait()
    for i in range(PER):
        lg = dot(images[i], router[...], 1, 0)
        logits.append(lg)
        ex = jnp.exp(lg - jnp.max(lg, axis=0, keepdims=True))
        p = ex / jnp.sum(ex, axis=0, keepdims=True)
        disp[i] = p
        parts.append(dot(p.astype(BF), images[i], 0, 0))
    sb_in[...] = pack(parts)
    pl.semaphore_wait(barrier, 2 * E - 1 + 2 * (NZ - 1))
    spread(sb_in, x_rows, 0)
    inputs[2].wait()
    parts = []
    for i in range(PER):
        lg = logits[i]
        ex = jnp.exp(lg - jnp.max(lg, axis=1, keepdims=True))
        p = ex / jnp.sum(ex, axis=1, keepdims=True)
        comb[i] = p
        parts.append(dot(p.astype(BF), out_grad[i], 0, 0))
    packed = pack(parts)
    for p in range(GP):
        sb_grad[p] = packed[:, :, p * GW: (p + 1) * GW]
    spread(sb_grad.at[0], g_rows.at[0], 1)
    has_left(sb_in, 0)
    has_left(sb_grad.at[0], 1)
    spread(sb_grad.at[1], g_rows.at[1], 2)
    spread(sb_grad.at[2], g_rows.at[2], 3)

    def xs():
        return x_rows[...].reshape(2 * ROWS, D)

    def forward(k, _):
        w_in_copy(k).wait()
        pre = dot(xs(), w_in[k], 1, 0)
        sq = pre * pre
        t = jnp.tanh(pre * (C0 + (C0 * C1) * sq))
        half = 0.5 * pre
        hid[k] = (half + half * t).astype(BF)
        gp[k] = (0.5 + 0.5 * t) + half * ((1.0 - t * t) * (C0 + (3.0 * C0 * C1) * sq))
        return 0

    def grad_out(k, p):
        g = dot(hid_t[k], g_rows[p].reshape(2 * ROWS, GW), 1, 0).astype(BF)
        gw_out[p, pl.ds(((1 - z // 4 + k) % 2) * (NZ // 2), NZ // 2)] = g.reshape(NZ // 2, CH_OUT, GW)

    def backward(k, part):
        rows = pl.ds(part * ROWS, ROWS)
        rows_g = jnp.concatenate([g_rows[p, part].reshape(ROWS, GW) for p in range(GP)], axis=1)
        dh = dot(rows_g, w_out[k], 1, 1)
        da[k, rows] = (dh * gp[k, rows]).astype(BF)

    def backward_own(k, _):
        backward(k, 0)
        return 0

    def grad_in(k, _):
        backward(k, 1)
        g = dot(xt[...], da[k], 1, 0)
        gw_in[:, tile_of(k)] = g.reshape(NZ, CH_IN, TILE).astype(BF)
        return 0

    def piece(which, part, c, way=None):
        if which == 0:
            return (part, c) if way is None else (part, c, pl.ds(way * (CH_OUT // 2), CH_OUT // 2))
        first = HALF_T * ((pair + part) % 2)
        return (c, pl.ds(first, HALF_T)) if way is None else (c, pl.ds(first + way, 1))

    def rs_copy(which, part, way, step):
        c = (z + 5 - step) % NZ if way == 0 else (z + 3 + step) % NZ
        mine, half, full = ((gw_out, ro_half, ro_full), (gw_in, ri_half, ri_full))[which]
        src = mine.at[piece(which, part, c, way if step == 1 else None)]
        dst = half.at[part, way] if step == 1 else full.at[part, way, step - 2]
        return pltpu.make_async_remote_copy(
            src_ref=src, dst_ref=dst,
            send_sem=rs_send.at[GP * which + part, way, step - 1], recv_sem=rs_recv.at[GP * which + part, way, step - 1],
            device_id=zdev(1 if way == 0 else NZ - 1), device_id_type=MESH,
        )

    sent = []

    def rs_send_on(which, part, way, step):
        n = len(sent) // 2 - IN_FLIGHT
        if n >= 0:
            rs_copy(*sent[2 * n + way]).wait_send()
        rs_copy(which, part, way, step).start()
        sent.append((which, part, way, step))

    def rs_start(which, part):
        for way in range(2):
            rs_send_on(which, part, way, 1)

    def rs_next(which, part, step):
        mine, half, full = ((gw_out, ro_half, ro_full), (gw_in, ri_half, ri_full))[which]
        for way in range(2):
            rs_copy(which, part, way, step).wait_recv()
            c = (z + 4 - step) % NZ if way == 0 else (z + 4 + step) % NZ
            here = piece(which, part, c, way if step == 1 else None)
            got = half[part, way] if step == 1 else full[part, way, step - 2]
            mine[here] = (mine[here].astype(F32) + got.astype(F32)).astype(BF)
            rs_send_on(which, part, way, step + 1)

    def rs_end(which, part):
        for way in range(2):
            rs_copy(which, part, way, 4).wait_recv()
        if which == 0:
            got = ro_full[part, 0, 2].astype(F32) + ro_full[part, 1, 2].astype(F32)
            w_out_share[:, part * GW: (part + 1) * GW] = (gw_out[part, z].astype(F32) + got).astype(BF)
        else:
            for n in range(HALF_T):
                t = HALF_T * ((pair + part) % 2) + n
                got = ri_full[part, 0, 2, n].astype(F32) + ri_full[part, 1, 2, n].astype(F32)
                cols = pl.ds(pl.multiple_of(t * TILE, TILE), TILE)
                w_in_share[:, cols] = (gw_in[z, t].astype(F32) + got).astype(BF)

    has_come(x_rows, 0)
    lax.fori_loop(0, HALF_T, forward, 0)
    for k in range(HALF_T):
        hid_t[k] = jnp.transpose(hid[k])
    has_come(g_rows.at[0], 1)
    grad_out(0, 0)
    rs_start(0, 0)
    grad_out(1, 0)
    lax.fori_loop(HALF_T, NT, forward, 0)
    off = pl.ds(pl.multiple_of(pair * (D // 2), 128), D // 2)
    xt[...] = jnp.transpose(x_rows[:, :, :, off].reshape(2 * ROWS, D // 2))
    acc = None
    for k in range(NT):
        w_out_copy(k).wait()
        part = dot(hid[k, :ROWS], w_out[k], 1, 0)
        acc = part if acc is None else acc + part
    so_send[...] = acc.astype(BF).reshape(E, BLK, D)
    rs_next(0, 0, 1)
    has_come(g_rows.at[1], 2)
    has_come(g_rows.at[2], 3)
    for p in (1, 2):
        grad_out(0, p)
        rs_start(0, p)
    back(so_send, so_home, 4)
    for p in (1, 2):
        grad_out(1, p)
    lax.fori_loop(0, NT, backward_own, 0)
    rs_next(0, 1, 1)
    acc = dot(da[0, :ROWS], w_in[0], 1, 1)
    for k in range(1, NT):
        acc = acc + dot(da[k, :ROWS], w_in[k], 1, 1)
    dx_send[...] = acc.astype(BF).reshape(E, BLK, D)
    back(dx_send, dx_home, 5)
    rs_next(0, 2, 1)
    lax.fori_loop(0, HALF_T, grad_in, 0)
    rs_start(1, 0)
    rs_next(0, 0, 2)
    lax.fori_loop(HALF_T, NT, grad_in, 0)
    rs_start(1, 1)
    rs_next(0, 1, 2)
    rs_next(0, 2, 2)

    def home(ref, i):
        return ref[...].astype(F32).reshape(E, PER, SPE, D)[:, i].reshape(S, D).astype(BF)

    wait_bytes(so_home, a2a_recv.at[4, 0])
    first = []
    for i in range(PER):
        dc = dot(out_grad[i], home(so_home, i), 1, 1)
        cm = comb[i]
        first.append(cm * (dc - jnp.sum(cm * dc, axis=1, keepdims=True)))
    wait_bytes(dx_home, a2a_recv.at[5, 0])
    rs_next(1, 0, 1)
    total = jnp.zeros((S, D), F32)
    for i in range(PER):
        dx = home(dx_home, i)
        dd = dot(images[i], dx, 1, 1)
        dm = disp[i]
        dl = (first[i] + dm * (dd - jnp.sum(dm * dd, axis=0, keepdims=True))).astype(BF)
        total = total + dot(dl, images[i], 0, 0)
        image_grad[i] = (dot(dm.astype(BF), dx, 1, 0) + dot(dl, router[...], 1, 1)).astype(BF)
    total = total.reshape(E, SPE, D)
    rpart[...] = jnp.concatenate([total[:, :, : D // 2], total[:, :, D // 2:]], axis=1).astype(BF)

    pltpu.make_async_copy(rpart.at[e], r_a.at[e], ar_recv.at[0]).start()

    def send_a(k, _):
        to = (e + k) % E
        pltpu.make_async_remote_copy(
            src_ref=rpart.at[to], dst_ref=r_a.at[e], send_sem=ar_send.at[0], recv_sem=ar_recv.at[0],
            device_id=(d, to), device_id_type=MESH,
        ).start()
        return 0

    lax.fori_loop(1, E, send_a, 0)
    rs_next(1, 1, 1)
    rs_next(0, 0, 3)
    wait_bytes(r_a, ar_recv.at[0])
    summed = jnp.sum(r_a[...].astype(F32), axis=0)
    for h in range(2):
        for r in range(SPE):
            b_rows[h * SPE + r] = summed[h * SPE + r: h * SPE + r + 1, :]

    def to_column(src_of, dst, n):
        pltpu.make_async_copy(src_of(pair, z), dst.at[pair, z], ar_recv.at[n]).start()
        for k in range(NZ):
            to = (z + k) % NZ
            if k:
                pltpu.make_async_remote_copy(
                    src_ref=src_of(pair, to), dst_ref=dst.at[pair, z], send_sem=ar_send.at[n], recv_sem=ar_recv.at[n],
                    device_id=zdev(k), device_id_type=MESH,
                ).start()
            pltpu.make_async_remote_copy(
                src_ref=src_of(1 - pair, to), dst_ref=dst.at[pair, z], send_sem=ar_send.at[n], recv_sem=ar_recv.at[n],
                device_id=zdev_other(k), device_id_type=MESH,
            ).start()

    to_column(lambda h, r: b_rows.at[h * NZ + r], r_b2, 1)
    rs_next(1, 0, 2)
    rs_next(0, 1, 3)
    wait_bytes(r_b2, ar_recv.at[1])
    c_row[0] = jnp.sum(r_b2[...].reshape(2 * NZ, 1, D // 2), axis=0)
    to_column(lambda h, r: c_row.at[0], r_b3, 2)
    rs_next(0, 2, 3)
    rs_next(1, 1, 2)
    wait_bytes(r_b3, ar_recv.at[2])
    for h in range(2):
        for r in range(SPE):
            c_mine[r:r + 1, h * (D // 2): (h + 1) * (D // 2)] = r_b3[h, r]
    pltpu.make_async_copy(c_mine, r_c.at[e], ar_recv.at[3]).start()

    def send_c(k, _):
        pltpu.make_async_remote_copy(
            src_ref=c_mine, dst_ref=r_c.at[e], send_sem=ar_send.at[3], recv_sem=ar_recv.at[3],
            device_id=(d, (e + k) % E), device_id_type=MESH,
        ).start()
        return 0

    lax.fori_loop(1, E, send_c, 0)
    rs_next(1, 0, 3)
    rs_next(1, 1, 3)
    for p in range(GP):
        rs_end(0, p)
    wait_bytes(r_c, ar_recv.at[3])
    router_grad[...] = r_c[...]
    rs_end(1, 0)
    rs_end(1, 1)

    has_left(sb_grad.at[1], 2)
    has_left(sb_grad.at[2], 3)
    for n in (4, 5):
        wait_bytes(so_send.at[pl.ds(0, E - 1)], a2a_send.at[n, 0])
    for last in sent[-2 * IN_FLIGHT:]:
        rs_copy(*last).wait_send()
    wait_bytes(rpart.at[pl.ds(0, E - 1)], ar_send.at[0])
    for n in (1, 2):
        wait_bytes(b_rows.at[pl.ds(0, 2 * NZ - 1)], ar_send.at[n])
    wait_bytes(r_c.at[pl.ds(0, E - 1)], ar_send.at[3])


def deliver(image_grad_in, router_grad_in, w_in_in, w_out_in, image_grad, router_grad, w_in_share, w_out_share, router_held, sem):
    copies = [
        pltpu.make_async_copy(image_grad_in, image_grad, sem.at[0]),
        pltpu.make_async_copy(w_in_in, w_in_share.at[0], sem.at[1]),
        pltpu.make_async_copy(w_out_in, w_out_share.at[0], sem.at[2]),
        pltpu.make_async_copy(router_held, router_grad, sem.at[3]),
    ]
    for c in copies[:3]:
        c.start()
    router_held[...] = jnp.transpose(router_grad_in[...].reshape(S, D))
    copies[3].start()
    for c in copies:
        c.wait()


def local(images, out_grad, router, w_in, w_out):
    hbm = pl.BlockSpec(memory_space=pltpu.HBM)
    vm = pl.BlockSpec(memory_space=pltpu.VMEM)
    V = pltpu.VMEM
    DMA = pltpu.SemaphoreType.DMA
    parts = pl.pallas_call(
        kernel,
        out_shape=(V((PER, M, D), BF), V((E, SPE, D), F32), V((CH_IN, H), BF), V((CH_OUT, D), BF)),
        in_specs=[hbm] * 5,
        out_specs=(vm,) * 4,
        scratch_shapes=[
            V((PER, M, D), BF), V((PER, M, D), BF), V((D, S), BF),
            V((NT, D, TILE), BF), V((NT, TILE, D), BF),
            V((PER, M, S), F32), V((PER, M, S), F32),
            V((E, BLK, D), BF), V((GP, E, BLK, GW), BF),
            V((2, E, BLK, D), BF), V((GP, 2, E, BLK, GW), BF),
            V((NT, 2 * ROWS, TILE), BF), V((HALF_T, TILE, 2 * ROWS), BF), V((NT, 2 * ROWS, TILE), F32), V((NT, 2 * ROWS, TILE), BF),
            V((D // 2, 2 * ROWS), BF),
            V((GP, NZ, CH_OUT, GW), BF), V((NZ, NT, CH_IN, TILE), BF),
            V((GP, 2, CH_OUT // 2, GW), BF), V((GP, 2, 3, CH_OUT, GW), BF),
            V((2, 2, 1, CH_IN, TILE), BF), V((2, 2, 3, HALF_T, CH_IN, TILE), BF),
            V((E, BLK, D), BF), V((E, BLK, D), BF), V((E, BLK, D), BF), V((E, BLK, D), BF),
            V((E, 2 * SPE, D // 2), BF), V((E, 2 * SPE, D // 2), BF),
            V((2 * NZ, 1, D // 2), F32), V((2, NZ, 1, D // 2), F32),
            V((1, 1, D // 2), F32), V((2, NZ, 1, D // 2), F32), V((SPE, D), F32), V((E, SPE, D), F32),
            DMA((2, NT)), DMA((3,)),
            DMA((6, 2)), DMA((6, 2)),
            DMA((GP + 2, 2, 4)), DMA((GP + 2, 2, 4)),
            DMA((4,)), DMA((4,)),
        ],
        compiler_params=pltpu.CompilerParams(
            collective_id=0, has_side_effects=True, vmem_limit_bytes=62 * 1024 * 1024
        ),
    )(images, out_grad, router, w_in[0], w_out[0])
    return pl.pallas_call(
        deliver,
        out_shape=(
            jax.ShapeDtypeStruct((PER, M, D), BF),
            jax.ShapeDtypeStruct((D, S), F32),
            jax.ShapeDtypeStruct((1, CH_IN, H), BF),
            jax.ShapeDtypeStruct((1, CH_OUT, D), BF),
        ),
        in_specs=[vm] * 4,
        out_specs=(hbm,) * 4,
        scratch_shapes=[V((D, S), F32), DMA((4,))],
        compiler_params=pltpu.CompilerParams(vmem_limit_bytes=16 * 1024 * 1024),
    )(*parts)


def solution(mesh):
    return jax.shard_map(
        local,
        mesh=mesh,
        in_specs=(
            P(("dp", "expert"), None, None),
            P(("dp", "expert"), None, None),
            P(),
            P("expert", None, None),
            P("expert", None, None),
        ),
        out_specs=(
            P(("dp", "expert"), None, None),
            P(),
            P("expert", "dp", None),
            P("expert", "dp", None),
        ),
        check_vma=False,
    )
```

```python
import math

import jax
import jax.numpy as jnp
from jax import lax
from jax.experimental import pallas as pl
from jax.experimental.pallas import tpu as pltpu
from jax.sharding import PartitionSpec as P

MESH = pl.DeviceIdType.MESH
BF = jnp.bfloat16
F32 = jnp.float32

D = 768
H = 3072
M = 256
S = 128
E = 16
NZ = 8
PER = 2
SPE = 8
BLK = PER * SPE
ROWS = E * BLK
TILE = 768
NT = H // TILE
HALF_T = NT // 2
GP = 3
GW = D // GP
IN_FLIGHT = 5
CH_IN = D // (2 * NZ)
CH_OUT = H // (2 * NZ)
C0 = math.sqrt(2.0 / math.pi)
C1 = 0.044715


def dot(a, b, ca, cb):
    return lax.dot_general(a, b, (((ca,), (cb,)), ((), ())), preferred_element_type=F32)


def kernel(
    images_hbm, out_grad_hbm, router_hbm, w_in_hbm, w_out_hbm,
    image_grad, router_grad, w_in_share, w_out_share,
    images, out_grad, router,
    w_in, w_out, disp, comb, sb_in, sb_grad, x_rows, g_rows,
    hid, hid_t, gp, da, xt, gw_out, gw_in,
    ro_half, ro_full, ri_half, ri_full,
    so_send, dx_send, so_home, dx_home,
    rpart, r_a, b_rows, r_b2, c_row, r_b3, c_mine, r_c,
    w_sem, io_sem, a2a_send, a2a_recv, rs_send, rs_recv, ar_send, ar_recv,
):
    d = lax.axis_index("dp")
    e = lax.axis_index("expert")
    pair = d // NZ
    z = d % NZ
    other_dp = (1 - pair) * NZ + z

    def zdev(k):
        return (pair * NZ + (z + k) % NZ, e)

    def zdev_other(k):
        return ((1 - pair) * NZ + (z + k) % NZ, e)

    inputs = [
        pltpu.make_async_copy(images_hbm, images, io_sem.at[0]),
        pltpu.make_async_copy(router_hbm, router, io_sem.at[1]),
        pltpu.make_async_copy(out_grad_hbm, out_grad, io_sem.at[2]),
    ]
    for c in inputs:
        c.start()

    barrier = pltpu.get_barrier_semaphore()

    def greet(k, _):
        pl.semaphore_signal(barrier, inc=1, device_id=(other_dp, (e + k) % E), device_id_type=MESH)
        return 0

    def greet_own(k, _):
        pl.semaphore_signal(barrier, inc=1, device_id=(d, (e + k) % E), device_id_type=MESH)
        return 0

    lax.fori_loop(0, E, greet, 0)
    lax.fori_loop(1, E, greet_own, 0)
    for k in range(1, NZ):
        pl.semaphore_signal(barrier, inc=1, device_id=zdev(k), device_id_type=MESH)
        pl.semaphore_signal(barrier, inc=1, device_id=zdev_other(k), device_id_type=MESH)

    def tile_of(k):
        return 2 * ((pair + k // 2) % 2) + (1 - z // 4 + k) % 2

    def w_in_copy(k):
        cols = pl.ds(pl.multiple_of(tile_of(k) * TILE, TILE), TILE)
        return pltpu.make_async_copy(w_in_hbm.at[:, cols], w_in.at[k], w_sem.at[0, k])

    def w_out_copy(k):
        rows = pl.ds(pl.multiple_of(tile_of(k) * TILE, TILE), TILE)
        return pltpu.make_async_copy(w_out_hbm.at[rows, :], w_out.at[k], w_sem.at[1, k])

    def spread(src, dst, n):
        pltpu.make_async_copy(src.at[e], dst.at[0, e], a2a_recv.at[n, 0]).start()

        def far(k, _):
            to = (e + k) % E
            pltpu.make_async_remote_copy(
                src_ref=src.at[to], dst_ref=dst.at[1, e],
                send_sem=a2a_send.at[n, 1], recv_sem=a2a_recv.at[n, 1],
                device_id=(other_dp, to), device_id_type=MESH,
            ).start()
            return 0

        def both(k, _):
            to = (e + k) % E
            pltpu.make_async_remote_copy(
                src_ref=src.at[to], dst_ref=dst.at[0, e],
                send_sem=a2a_send.at[n, 0], recv_sem=a2a_recv.at[n, 0],
                device_id=(d, to), device_id_type=MESH,
            ).start()
            return far(k, 0)

        far(0, 0)
        lax.fori_loop(1, E, both, 0)

    def has_left(src, n):
        wait_bytes(src.at[pl.ds(0, E - 1)], a2a_send.at[n, 0])
        wait_bytes(src, a2a_send.at[n, 1])

    def has_come(dst, n):
        wait_bytes(dst.at[0], a2a_recv.at[n, 0])
        wait_bytes(dst.at[1], a2a_recv.at[n, 1])

    def wait_bytes(ref, sem):
        pltpu.make_async_copy(ref, ref, sem).wait()

    def back(src, dst, n):
        pltpu.make_async_copy(src.at[e], dst.at[e], a2a_recv.at[n, 0]).start()

        def near(k, _):
            to = (e + k) % E
            pltpu.make_async_remote_copy(
                src_ref=src.at[to], dst_ref=dst.at[e],
                send_sem=a2a_send.at[n, 0], recv_sem=a2a_recv.at[n, 0],
                device_id=(d, to), device_id_type=MESH,
            ).start()
            return 0

        lax.fori_loop(1, E, near, 0)

    def pack(parts):
        parts = [p.reshape(E, SPE, D) for p in parts]
        return jnp.concatenate(parts, axis=1).astype(BF)

    parts = []
    logits = []
    inputs[1].wait()
    inputs[0].wait()
    inputs[2].wait()
    for k in range(NT):
        w_in_copy(k).start()
    for k in range(NT):
        w_out_copy(k).start()
    for i in range(PER):
        lg = dot(images[i], router[...], 1, 0)
        logits.append(lg)
        ex = jnp.exp(lg - jnp.max(lg, axis=0, keepdims=True))
        p = ex / jnp.sum(ex, axis=0, keepdims=True)
        disp[i] = p
        parts.append(dot(p.astype(BF), images[i], 0, 0))
    sb_in[...] = pack(parts)
    pl.semaphore_wait(barrier, 2 * E - 1 + 2 * (NZ - 1))
    spread(sb_in, x_rows, 0)
    parts = []
    for i in range(PER):
        lg = logits[i]
        ex = jnp.exp(lg - jnp.max(lg, axis=1, keepdims=True))
        p = ex / jnp.sum(ex, axis=1, keepdims=True)
        comb[i] = p
        parts.append(dot(p.astype(BF), out_grad[i], 0, 0))
    packed = pack(parts)
    for p in range(GP):
        sb_grad[p] = packed[:, :, p * GW: (p + 1) * GW]
    spread(sb_grad.at[0], g_rows.at[0], 1)
    has_left(sb_in, 0)
    has_left(sb_grad.at[0], 1)
    spread(sb_grad.at[1], g_rows.at[1], 2)
    spread(sb_grad.at[2], g_rows.at[2], 3)

    def xs():
        return x_rows[...].reshape(2 * ROWS, D)

    def forward(k, _):
        w_in_copy(k).wait()
        pre = dot(xs(), w_in[k], 1, 0)
        sq = pre * pre
        t = jnp.tanh(pre * (C0 + (C0 * C1) * sq))
        half = 0.5 * pre
        hid[k] = (half + half * t).astype(BF)
        gp[k] = (0.5 + 0.5 * t) + half * ((1.0 - t * t) * (C0 + (3.0 * C0 * C1) * sq))
        return 0

    def grad_out(k, p):
        g = dot(hid_t[k], g_rows[p].reshape(2 * ROWS, GW), 1, 0).astype(BF)
        gw_out[p, pl.ds(((1 - z // 4 + k) % 2) * (NZ // 2), NZ // 2)] = g.reshape(NZ // 2, CH_OUT, GW)

    def backward(k, part):
        rows = pl.ds(part * ROWS, ROWS)
        rows_g = jnp.concatenate([g_rows[p, part].reshape(ROWS, GW) for p in range(GP)], axis=1)
        dh = dot(rows_g, w_out[k], 1, 1)
        da[k, rows] = (dh * gp[k, rows]).astype(BF)

    def backward_own(k, _):
        backward(k, 0)
        return 0

    def grad_in(k, _):
        backward(k, 1)
        g = dot(xt[...], da[k], 1, 0)
        gw_in[:, tile_of(k)] = g.reshape(NZ, CH_IN, TILE).astype(BF)
        return 0

    def piece(which, part, c, way=None):
        if which == 0:
            return (part, c) if way is None else (part, c, pl.ds(way * (CH_OUT // 2), CH_OUT // 2))
        first = HALF_T * ((pair + part) % 2)
        return (c, pl.ds(first, HALF_T)) if way is None else (c, pl.ds(first + way, 1))

    def rs_copy(which, part, way, step):
        c = (z + 5 - step) % NZ if way == 0 else (z + 3 + step) % NZ
        mine, half, full = ((gw_out, ro_half, ro_full), (gw_in, ri_half, ri_full))[which]
        src = mine.at[piece(which, part, c, way if step == 1 else None)]
        dst = half.at[part, way] if step == 1 else full.at[part, way, step - 2]
        return pltpu.make_async_remote_copy(
            src_ref=src, dst_ref=dst,
            send_sem=rs_send.at[GP * which + part, way, step - 1], recv_sem=rs_recv.at[GP * which + part, way, step - 1],
            device_id=zdev(1 if way == 0 else NZ - 1), device_id_type=MESH,
        )

    sent = []

    def rs_send_on(which, part, way, step):
        n = len(sent) // 2 - IN_FLIGHT
        if n >= 0:
            rs_copy(*sent[2 * n + way]).wait_send()
        rs_copy(which, part, way, step).start()
        sent.append((which, part, way, step))

    def rs_start(which, part):
        for way in range(2):
            rs_send_on(which, part, way, 1)

    def rs_next(which, part, step):
        mine, half, full = ((gw_out, ro_half, ro_full), (gw_in, ri_half, ri_full))[which]
        for way in range(2):
            rs_copy(which, part, way, step).wait_recv()
            c = (z + 4 - step) % NZ if way == 0 else (z + 4 + step) % NZ
            here = piece(which, part, c, way if step == 1 else None)
            got = half[part, way] if step == 1 else full[part, way, step - 2]
            mine[here] = (mine[here].astype(F32) + got.astype(F32)).astype(BF)
            rs_send_on(which, part, way, step + 1)

    def rs_end(which, part):
        for way in range(2):
            rs_copy(which, part, way, 4).wait_recv()
        if which == 0:
            got = ro_full[part, 0, 2].astype(F32) + ro_full[part, 1, 2].astype(F32)
            w_out_share[:, part * GW: (part + 1) * GW] = (gw_out[part, z].astype(F32) + got).astype(BF)
        else:
            for n in range(HALF_T):
                t = HALF_T * ((pair + part) % 2) + n
                got = ri_full[part, 0, 2, n].astype(F32) + ri_full[part, 1, 2, n].astype(F32)
                cols = pl.ds(pl.multiple_of(t * TILE, TILE), TILE)
                w_in_share[:, cols] = (gw_in[z, t].astype(F32) + got).astype(BF)

    has_come(x_rows, 0)
    lax.fori_loop(0, HALF_T, forward, 0)
    for k in range(HALF_T):
        hid_t[k] = jnp.transpose(hid[k])
    has_come(g_rows.at[0], 1)
    grad_out(0, 0)
    rs_start(0, 0)
    grad_out(1, 0)
    lax.fori_loop(HALF_T, NT, forward, 0)
    off = pl.ds(pl.multiple_of(pair * (D // 2), 128), D // 2)
    xt[...] = jnp.transpose(x_rows[:, :, :, off].reshape(2 * ROWS, D // 2))
    acc = None
    for k in range(NT):
        w_out_copy(k).wait()
        part = dot(hid[k, :ROWS], w_out[k], 1, 0)
        acc = part if acc is None else acc + part
    so_send[...] = acc.astype(BF).reshape(E, BLK, D)
    rs_next(0, 0, 1)
    has_come(g_rows.at[1], 2)
    has_come(g_rows.at[2], 3)
    for p in (1, 2):
        grad_out(0, p)
        rs_start(0, p)
    back(so_send, so_home, 4)
    for p in (1, 2):
        grad_out(1, p)
    lax.fori_loop(0, NT, backward_own, 0)
    rs_next(0, 1, 1)
    acc = dot(da[0, :ROWS], w_in[0], 1, 1)
    for k in range(1, NT):
        acc = acc + dot(da[k, :ROWS], w_in[k], 1, 1)
    dx_send[...] = acc.astype(BF).reshape(E, BLK, D)
    back(dx_send, dx_home, 5)
    rs_next(0, 2, 1)
    lax.fori_loop(0, HALF_T, grad_in, 0)
    rs_start(1, 0)
    rs_next(0, 0, 2)
    lax.fori_loop(HALF_T, NT, grad_in, 0)
    rs_start(1, 1)
    rs_next(0, 1, 2)
    rs_next(0, 2, 2)

    def home(ref, i):
        return ref[...].astype(F32).reshape(E, PER, SPE, D)[:, i].reshape(S, D).astype(BF)

    wait_bytes(so_home, a2a_recv.at[4, 0])
    first = []
    for i in range(PER):
        dc = dot(out_grad[i], home(so_home, i), 1, 1)
        cm = comb[i]
        first.append(cm * (dc - jnp.sum(cm * dc, axis=1, keepdims=True)))
    wait_bytes(dx_home, a2a_recv.at[5, 0])
    rs_next(1, 0, 1)
    total = jnp.zeros((S, D), F32)
    for i in range(PER):
        dx = home(dx_home, i)
        dd = dot(images[i], dx, 1, 1)
        dm = disp[i]
        dl = (first[i] + dm * (dd - jnp.sum(dm * dd, axis=0, keepdims=True))).astype(BF)
        total = total + dot(dl, images[i], 0, 0)
        image_grad[i] = (dot(dm.astype(BF), dx, 1, 0) + dot(dl, router[...], 1, 1)).astype(BF)
    total = total.reshape(E, SPE, D)
    rpart[...] = jnp.concatenate([total[:, :, : D // 2], total[:, :, D // 2:]], axis=1).astype(BF)

    pltpu.make_async_copy(rpart.at[e], r_a.at[e], ar_recv.at[0]).start()

    def send_a(k, _):
        to = (e + k) % E
        pltpu.make_async_remote_copy(
            src_ref=rpart.at[to], dst_ref=r_a.at[e], send_sem=ar_send.at[0], recv_sem=ar_recv.at[0],
            device_id=(d, to), device_id_type=MESH,
        ).start()
        return 0

    lax.fori_loop(1, E, send_a, 0)
    rs_next(1, 1, 1)
    rs_next(0, 0, 3)
    wait_bytes(r_a, ar_recv.at[0])
    summed = jnp.sum(r_a[...].astype(F32), axis=0)
    for h in range(2):
        for r in range(SPE):
            b_rows[h * SPE + r] = summed[h * SPE + r: h * SPE + r + 1, :]

    def to_column(src_of, dst, n):
        pltpu.make_async_copy(src_of(pair, z), dst.at[pair, z], ar_recv.at[n]).start()
        for k in range(NZ):
            to = (z + k) % NZ
            if k:
                pltpu.make_async_remote_copy(
                    src_ref=src_of(pair, to), dst_ref=dst.at[pair, z], send_sem=ar_send.at[n], recv_sem=ar_recv.at[n],
                    device_id=zdev(k), device_id_type=MESH,
                ).start()
            pltpu.make_async_remote_copy(
                src_ref=src_of(1 - pair, to), dst_ref=dst.at[pair, z], send_sem=ar_send.at[n], recv_sem=ar_recv.at[n],
                device_id=zdev_other(k), device_id_type=MESH,
            ).start()

    to_column(lambda h, r: b_rows.at[h * NZ + r], r_b2, 1)
    rs_next(1, 0, 2)
    rs_next(0, 1, 3)
    wait_bytes(r_b2, ar_recv.at[1])
    c_row[0] = jnp.sum(r_b2[...].reshape(2 * NZ, 1, D // 2), axis=0)
    to_column(lambda h, r: c_row.at[0], r_b3, 2)
    rs_next(0, 2, 3)
    rs_next(1, 1, 2)
    wait_bytes(r_b3, ar_recv.at[2])
    for h in range(2):
        for r in range(SPE):
            c_mine[r:r + 1, h * (D // 2): (h + 1) * (D // 2)] = r_b3[h, r]
    pltpu.make_async_copy(c_mine, r_c.at[e], ar_recv.at[3]).start()

    def send_c(k, _):
        pltpu.make_async_remote_copy(
            src_ref=c_mine, dst_ref=r_c.at[e], send_sem=ar_send.at[3], recv_sem=ar_recv.at[3],
            device_id=(d, (e + k) % E), device_id_type=MESH,
        ).start()
        return 0

    lax.fori_loop(1, E, send_c, 0)
    rs_next(1, 0, 3)
    rs_next(1, 1, 3)
    for p in range(GP):
        rs_end(0, p)
    wait_bytes(r_c, ar_recv.at[3])
    router_grad[...] = r_c[...]
    rs_end(1, 0)
    rs_end(1, 1)

    has_left(sb_grad.at[1], 2)
    has_left(sb_grad.at[2], 3)
    for n in (4, 5):
        wait_bytes(so_send.at[pl.ds(0, E - 1)], a2a_send.at[n, 0])
    for last in sent[-2 * IN_FLIGHT:]:
        rs_copy(*last).wait_send()
    wait_bytes(rpart.at[pl.ds(0, E - 1)], ar_send.at[0])
    for n in (1, 2):
        wait_bytes(b_rows.at[pl.ds(0, 2 * NZ - 1)], ar_send.at[n])
    wait_bytes(r_c.at[pl.ds(0, E - 1)], ar_send.at[3])


def deliver(image_grad_in, router_grad_in, w_in_in, w_out_in, image_grad, router_grad, w_in_share, w_out_share, router_held, sem):
    copies = [
        pltpu.make_async_copy(image_grad_in, image_grad, sem.at[0]),
        pltpu.make_async_copy(w_in_in, w_in_share.at[0], sem.at[1]),
        pltpu.make_async_copy(w_out_in, w_out_share.at[0], sem.at[2]),
        pltpu.make_async_copy(router_held, router_grad, sem.at[3]),
    ]
    for c in copies[:3]:
        c.start()
    router_held[...] = jnp.transpose(router_grad_in[...].reshape(S, D))
    copies[3].start()
    for c in copies:
        c.wait()


def local(images, out_grad, router, w_in, w_out):
    hbm = pl.BlockSpec(memory_space=pltpu.HBM)
    vm = pl.BlockSpec(memory_space=pltpu.VMEM)
    V = pltpu.VMEM
    DMA = pltpu.SemaphoreType.DMA
    parts = pl.pallas_call(
        kernel,
        out_shape=(V((PER, M, D), BF), V((E, SPE, D), F32), V((CH_IN, H), BF), V((CH_OUT, D), BF)),
        in_specs=[hbm] * 5,
        out_specs=(vm,) * 4,
        scratch_shapes=[
            V((PER, M, D), BF), V((PER, M, D), BF), V((D, S), BF),
            V((NT, D, TILE), BF), V((NT, TILE, D), BF),
            V((PER, M, S), F32), V((PER, M, S), F32),
            V((E, BLK, D), BF), V((GP, E, BLK, GW), BF),
            V((2, E, BLK, D), BF), V((GP, 2, E, BLK, GW), BF),
            V((NT, 2 * ROWS, TILE), BF), V((HALF_T, TILE, 2 * ROWS), BF), V((NT, 2 * ROWS, TILE), F32), V((NT, 2 * ROWS, TILE), BF),
            V((D // 2, 2 * ROWS), BF),
            V((GP, NZ, CH_OUT, GW), BF), V((NZ, NT, CH_IN, TILE), BF),
            V((GP, 2, CH_OUT // 2, GW), BF), V((GP, 2, 3, CH_OUT, GW), BF),
            V((2, 2, 1, CH_IN, TILE), BF), V((2, 2, 3, HALF_T, CH_IN, TILE), BF),
            V((E, BLK, D), BF), V((E, BLK, D), BF), V((E, BLK, D), BF), V((E, BLK, D), BF),
            V((E, 2 * SPE, D // 2), BF), V((E, 2 * SPE, D // 2), BF),
            V((2 * NZ, 1, D // 2), F32), V((2, NZ, 1, D // 2), F32),
            V((1, 1, D // 2), F32), V((2, NZ, 1, D // 2), F32), V((SPE, D), F32), V((E, SPE, D), F32),
            DMA((2, NT)), DMA((3,)),
            DMA((6, 2)), DMA((6, 2)),
            DMA((GP + 2, 2, 4)), DMA((GP + 2, 2, 4)),
            DMA((4,)), DMA((4,)),
        ],
        compiler_params=pltpu.CompilerParams(
            collective_id=0, has_side_effects=True, vmem_limit_bytes=62 * 1024 * 1024
        ),
    )(images, out_grad, router, w_in[0], w_out[0])
    return pl.pallas_call(
        deliver,
        out_shape=(
            jax.ShapeDtypeStruct((PER, M, D), BF),
            jax.ShapeDtypeStruct((D, S), F32),
            jax.ShapeDtypeStruct((1, CH_IN, H), BF),
            jax.ShapeDtypeStruct((1, CH_OUT, D), BF),
        ),
        in_specs=[vm] * 4,
        out_specs=(hbm,) * 4,
        scratch_shapes=[V((D, S), F32), DMA((4,))],
        compiler_params=pltpu.CompilerParams(vmem_limit_bytes=16 * 1024 * 1024),
    )(*parts)


def solution(mesh):
    return jax.shard_map(
        local,
        mesh=mesh,
        in_specs=(
            P(("dp", "expert"), None, None),
            P(("dp", "expert"), None, None),
            P(),
            P("expert", None, None),
            P("expert", None, None),
        ),
        out_specs=(
            P(("dp", "expert"), None, None),
            P(),
            P("expert", "dp", None),
            P("expert", "dp", None),
        ),
        check_vma=False,
    )
```
